32 devices in a mesh: row: 4 (over z), col: 8 (over y, x, core).
Axes of the slice: x: 2, y: 2, z: 4, core: 2. Of those that a mesh axis runs over, the one named last changes fastest.
Arguments:
- a_matrix: float32 [1024, 3072], P('row', 'col'), may hold values from -6 to 6
- b_matrix: float32 [1024, 3072], P('row', 'col'), as said below
Outputs:
- a_result: float32 [1024, 3072], P('row', 'col')
- b_result: float32 [1024, 3072], P('row', 'col')
The draws below stay inside these ranges and needn't reach their ends.
Inputs may be any that keep to these rules, and one draw needn't show every extreme that they name: b_matrix is zero in its first 256 columns and, at the window's columns t, zero in rows below t; its entry in row t at window column t lies between 4 and 8.
All inputs are finite; a program needn't handle non-finite values.
Results may differ from the reference program's by a relative error of at most 0.00023.
Values sent between devices are 32-bit elements; how exact they have to be, the bound alone decides.
A program may use at most 64 MiB of HBM per device.

```python
import math
import jax
import jax.numpy as jnp
from jax import lax

NB = 256
CB = 384
M = 1024
NCOLS = 3072
N_COL = 8


def draw_b_matrix(key, part):
    noise_key = jax.random.fold_in(key, 11)
    diag_key = jax.random.fold_in(key, 23)
    scale = 1.5 / math.sqrt(M)
    noise = jnp.clip(jax.random.normal(noise_key, (M, NCOLS), jnp.float32), -4.0, 4.0)
    noise = noise * scale
    diagonal = 4.0 * jnp.exp(jnp.log(2.0) * jax.random.uniform(diag_key, (M, 1), jnp.float32))
    width_dev = M // N_COL
    rows = jnp.arange(M)[:, None]
    columns = jnp.arange(NCOLS)[None, :]
    local = columns % CB
    inside = local >= CB - width_dev
    position = columns // CB * width_dev + local - (CB - width_dev)
    values = jnp.where(inside & (position == rows), diagonal, noise)
    values = jnp.where(inside & (position < rows), 0.0, values)
    values = jnp.where(columns < NB, 0.0, values)
    return values.astype(jnp.float32)


def shard_levels(key, dims, pieces, smallest, high):
    level, own = 1.0, jax.random.fold_in(key, 6)
    for dim, shards_of in pieces:
        heights = jnp.exp(jax.random.uniform(jax.random.fold_in(own, dim), (shards_of,), jnp.float32, smallest / len(pieces), high / len(pieces)))
        level = level * jnp.repeat(heights, dims[dim] // shards_of).reshape([-1 if axis == dim else 1 for axis in range(len(dims))])
    return level


def gaussian(key, shape, deviation, limit, shards=(), kind=jnp.bfloat16):
    level = shard_levels(key, shape, shards, -0.22, 0.18) if shards else 1.0
    drawn = jax.random.normal(key, shape, jnp.float32) * deviation * level
    return jnp.minimum(jnp.maximum(drawn, -limit), limit).astype(kind)


def setup_inputs(seed: int = 0) -> dict:
    key_list = jax.random.split(jax.random.key(seed), 3)
    a_matrix = gaussian(key_list[0], (M, NCOLS), 1.0, 6.0, ((0, 4), (1, 8)), jnp.float32)
    b_matrix = draw_b_matrix(jax.random.fold_in(key_list[2], 71), 0)
    return dict(a_matrix=a_matrix, b_matrix=b_matrix)


def product(left_side, right_side):
    return jnp.dot(left_side.astype(jnp.float32), right_side.astype(jnp.float32), precision=lax.Precision.HIGHEST, preferred_element_type=jnp.float32)

def tri_solve(factor, values, on_left, transpose):
    return lax.linalg.triangular_solve(factor, values, left_side=on_left, lower=True, transpose_a=transpose)

def inverse_of(square):
    normal = product(square.T, square)
    factor = jnp.linalg.cholesky(normal)
    first = tri_solve(factor, square.T, True, False)
    return tri_solve(factor, first, True, True)

def lower_from_reversed(gram):
    factor = jnp.linalg.cholesky(gram[::-1, ::-1])
    return factor.T[::-1, ::-1]

def reference(a_matrix, b_matrix):
    identity = jnp.eye(NB, dtype=jnp.float32)
    panel = a_matrix[:, :NB]
    factor = jnp.linalg.cholesky(product(panel.T, panel))
    q_panel = tri_solve(factor, panel, False, True)
    w_left = q_panel.at[:NB].add(identity)
    k_left = inverse_of(identity + q_panel[:NB])
    a_left = a_matrix - product(w_left, product(k_left, product(w_left.T, a_matrix)))
    b_left = b_matrix - product(w_left, product(k_left, product(w_left.T, b_matrix)))
    width_dev = M // N_COL
    positions = jnp.arange(M, dtype=jnp.int32)
    window_cols = (positions // width_dev * CB + (CB - width_dev) + positions % width_dev).astype(jnp.int32)
    strip = jnp.take(b_left[M - NB:], window_cols, axis=1)
    right_factor = lower_from_reversed(product(strip, strip.T))
    q_strip = tri_solve(right_factor, strip.T, False, False)
    w_right = q_strip.at[M - NB:].add(identity)
    k_right = inverse_of(identity + q_strip[M - NB:].T)
    results = []
    for current in (a_left, b_left):
        window = jnp.take(current, window_cols, axis=1)
        window = window - product(product(product(window, w_right), k_right), w_right.T)
        results.append(current.at[:, window_cols].set(window))
    return (results[0], results[1])
```

```python
import functools

import jax
import jax.numpy as jnp
from jax import lax
from jax.experimental import pallas as pl
from jax.experimental.pallas import tpu as pltpu
from jax.sharding import PartitionSpec as P

NB = 256
HB = NB // 2
TILE = 8
COUNT = HB // TILE
MESH = pl.DeviceIdType.MESH
VM = pl.BlockSpec(memory_space=pltpu.VMEM)
LIMIT = 56 * 1024 * 1024


def dot(x, y, cx=1, cy=0):
    return lax.dot_general(
        x,
        y,
        (((cx,), (cy,)), ((), ())),
        precision=lax.Precision.HIGHEST,
        preferred_element_type=jnp.float32,
    )


def spread(x):
    return jnp.broadcast_to(x, (TILE, HB))


def stack(rows):
    sub = lax.broadcasted_iota(jnp.int32, (TILE, HB), 0)
    out = rows[0]
    for k in range(1, TILE):
        out = jnp.where(sub == k, rows[k], out)
    return out


def apply_tile(tile, t, rows, inside):
    out = jnp.where(inside, 0.0, tile)
    for k in range(TILE):
        out = out - spread(tile[:, t * TILE + k : t * TILE + k + 1]) * rows[k]
    return out


def step(tiles, t, order, symmetric):
    lane = lax.broadcasted_iota(jnp.int32, (TILE, HB), 1) - t * TILE
    inside = (lane >= 0) & (lane < TILE)
    at = [lane == k for k in range(TILE)]
    place = {m: i for i, m in enumerate(order)}
    used = lambda r, k: not symmetric or place[r] <= place[k]
    rows = [spread(tiles[t][k : k + 1, :]) for k in range(TILE)]
    s = [
        [spread(rows[r][:, t * TILE + k : t * TILE + k + 1]) if used(r, k) else None for k in range(TILE)]
        for r in range(TILE)
    ]
    rows = [jnp.where(inside, jnp.where(at[k], 1.0, 0.0), rows[k]) for k in range(TILE)]
    forward = [None] * TILE
    for i, m in enumerate(order):
        later = order[i + 1 :]
        if symmetric:
            kept = jnp.where(at[m], s[m][m], rows[m])
            for k in later:
                kept = jnp.where(at[k], s[m][k], kept)
            forward[m] = kept
        inv = 1.0 / s[m][m]
        lead = {r: s[m][r] if symmetric else s[r][m] for r in later}
        for k in later:
            s[m][k] = s[m][k] * inv
        for r in later:
            for k in later:
                if used(r, k):
                    s[r][k] = s[r][k] - lead[r] * s[m][k]
        rows[m] = rows[m] * inv
        for r in later:
            rows[r] = rows[r] - lead[r] * rows[m]
        yield None
    for i in range(TILE - 1, 0, -1):
        m = order[i]
        for r in order[:i]:
            rows[r] = rows[r] - s[r][m] * rows[m]
    yield rows, forward, inside


def invert_half(a, reverse):
    tiles = [a[i * TILE : (i + 1) * TILE, :] for i in range(COUNT)]
    order, places = list(range(TILE)), list(range(COUNT))
    if reverse:
        order, places = order[::-1], places[::-1]
    for n, t in enumerate(places):
        for out in step(tiles, t, order, False):
            yield None
        rows, _, inside = out
        new = list(tiles)
        for i in places[n + 1 :] + places[: n + 1]:
            new[i] = stack(rows) if i == t else apply_tile(tiles[i], t, rows, inside)
        tiles = new
        yield None
    yield jnp.concatenate(tiles, axis=0)


def eliminate_half(a, reverse):
    tiles = [a[i * TILE : (i + 1) * TILE, :] for i in range(COUNT)]
    order, places = list(range(TILE)), list(range(COUNT))
    if reverse:
        order, places = order[::-1], places[::-1]
    for n, t in enumerate(places):
        for out in step(tiles, t, order, True):
            yield None
        rows, forward, inside = out
        tiles[t] = stack(forward)
        for i in places[n + 1 :]:
            tiles[i] = apply_tile(tiles[i], t, rows, inside)
        yield None
    a = jnp.concatenate(tiles, axis=0)
    rows = lax.broadcasted_iota(jnp.int32, (HB, HB), 0)
    cols = lax.broadcasted_iota(jnp.int32, (HB, HB), 1)
    diag = jnp.sum(jnp.where(rows == cols, a, 0.0), axis=1, keepdims=True)
    scale = 1.0 / jnp.sqrt(diag)
    keep = rows >= cols if reverse else rows <= cols
    factor = jnp.where(keep, a, 0.0) * scale
    yield factor, jnp.where(keep, jnp.where(rows == cols, 1.0, 0.0), a) * scale


def together(*chains):
    results, live = [None] * len(chains), list(range(len(chains)))
    while live:
        for j in list(live):
            value = next(chains[j], live)
            if value is live:
                live.remove(j)
            elif value is not None:
                results[j] = value
    return results


class Solve:
    def __init__(self, reverse):
        self.reverse = reverse
        self.p, self.q = (1, 0) if reverse else (0, 1)

    def cut(self, x, r, c):
        return x[r * HB : (r + 1) * HB, c * HB : (c + 1) * HB]

    def first(self, gram):
        p = self.p
        ((self.fpp, self.ipp),) = together(eliminate_half(self.cut(gram, p, p), self.reverse))

    def second(self, gram, top):
        p, q = self.p, self.q
        self.rpq = dot(self.ipp, self.cut(gram, p, q))
        rest = self.cut(gram, q, q) - dot(self.rpq, self.rpq, 0, 0)
        (self.fqq, self.iqq), self.inv = together(
            eliminate_half(rest, self.reverse),
            invert_half(self.cut(top, p, p) + self.fpp, self.reverse),
        )
        self.fqp = self.cut(top, q, p)
        self.k = dot(self.inv, self.cut(top, p, q) + self.rpq)
        self.rest = self.cut(top, q, q) + self.fqq - dot(self.fqp, self.k)

    def third(self):
        (self.sinv,) = together(invert_half(self.rest, self.reverse))

    def factor(self):
        zero = jnp.zeros((HB, HB), jnp.float32)
        if self.reverse:
            blocks = [[self.fqq, zero], [self.rpq, self.fpp]]
        else:
            blocks = [[self.fpp, self.rpq], [zero, self.fqq]]
        return jnp.concatenate([jnp.concatenate(b, axis=1) for b in blocks], axis=0)

    def prepare(self, y, t):
        half = lambda x, i: x[:, i * HB : (i + 1) * HB]
        yp = dot(half(y, self.p), self.ipp, 1, 1)
        yq = dot(half(y, self.q) - dot(yp, self.rpq), self.iqq, 1, 1)
        hp = dot(yp + half(t, self.p), self.inv, 1, 1)
        return hp, yq + half(t, self.q) - dot(hp, self.fqp, 1, 1)

    def finish(self, hp, hq):
        cq = dot(hq, self.sinv, 1, 1)
        cp = hp - dot(cq, self.k, 1, 1)
        return jnp.concatenate([cq, cp] if self.reverse else [cp, cq], axis=1)


def send(source, target, send_sem, recv_sem, peer):
    copy = pltpu.make_async_remote_copy(
        src_ref=source,
        dst_ref=target,
        send_sem=send_sem,
        recv_sem=recv_sem,
        device_id=peer,
        device_id_type=MESH,
    )
    return copy


def start_all(axis, n, me, source, target, sems):
    copies = []
    for d in range(1, n):
        peer = lax.rem(me + d, n)
        copy = send(source(peer), target, sems[0].at[d - 1], sems[1].at[d - 1], {axis: peer})
        copy.start()
        copies.append(copy)
    return copies


def wait_all(copies):
    for copy in copies:
        copy.wait()


class Pairs:
    def __init__(self, n, me, slot, sems):
        self.n, self.me, self.slot, self.sems = n, me, slot, sems
        self.partner = me + 1 - 2 * lax.rem(me, 2)

    def copy(self, index, block, peer):
        ref = self.slot(block)
        copy = send(ref, ref, self.sems[0].at[index], self.sems[1].at[index], {"col": peer})
        copy.start()
        return copy

    def start(self):
        half = self.n // 2
        self.far = [
            self.copy(d - 1, self.me, lax.rem(self.me + 2 * d, self.n)) for d in range(1, half)
        ]
        self.near = [self.copy(half - 1, self.me, self.partner)]

    def forward(self):
        half = self.n // 2
        for d in range(1, half):
            self.far[d - 1].wait_recv()
            block = lax.rem(self.me + self.n - 2 * d, self.n)
            self.near.append(self.copy(half - 1 + d, block, self.partner))

    def wait(self):
        for copy in self.far:
            copy.wait_send()
        wait_all(self.near)


def kernel(n_row, n_col, a_ref, b_ref, oa_ref, ob_ref, *scratch):
    panel, bw, aw, turned, other, coefs, strips, own_y, got_y, own_c, got_c, both, r_ref = scratch[:13]
    pairs_of_sems = [scratch[i : i + 2] for i in range(13, len(scratch), 2)]
    s_scatter, s_row, s_panel, s_bw, s_aw, s_other, s_coefs, s_strips, s_y, s_c, s_both = pairs_of_sems
    rows, cols = a_ref.shape
    window = strips.shape[1]
    start = cols - window
    chunk = rows // n_col
    n_last = NB // window
    row, col = lax.axis_index("row"), lax.axis_index("col")

    barrier = pltpu.get_barrier_semaphore()
    for axis, n, me in (("row", n_row, row), ("col", n_col, col)):
        for d in range(1, n):
            pl.semaphore_signal(
                barrier, inc=1, device_id={axis: lax.rem(me + d, n)}, device_id_type=MESH
            )
    pl.semaphore_wait(barrier, n_row + n_col - 2)

    def part(c):
        return panel.at[row, pl.ds(c * chunk, chunk)]

    def scatter(c):
        source = a_ref.at[pl.ds(c * chunk, chunk), pl.ds(0, NB)]
        return send(source, part(c), s_scatter[0].at[c - 1], s_scatter[1].at[0], {"col": c})

    @pl.when(col == 0)
    def _():
        for c in range(1, n_col):
            scatter(c).start()
        panel[row, pl.ds(0, chunk)] = a_ref[:chunk, :NB]

    bw[row] = b_ref[:, start:].T
    aw[row] = a_ref[:, start:].T
    turned[...] = jnp.concatenate([a_ref[:, :start].T, b_ref[:, :start].T], axis=0).reshape(
        turned.shape
    )
    other[row] = turned[row]

    @pl.when(col != 0)
    def _():
        send(part(col), part(col), s_scatter[0].at[0], s_scatter[1].at[0], {"col": 0}).wait_recv()

    mine = part(col)
    chunks = start_all("row", n_row, row, lambda peer: mine, mine, s_row)
    sent_bw = start_all("row", n_row, row, lambda peer: bw.at[row], bw.at[row], s_bw)
    wait_all(chunks)
    spread_panel = Pairs(n_col, col, lambda c: panel.at[:, pl.ds(c * chunk, chunk)], s_panel)
    spread_panel.start()
    spread_panel.forward()
    spread_panel.wait()

    @pl.when(col == 0)
    def _():
        for c in range(1, n_col):
            scatter(c).wait_send()

    square = jnp.zeros((NB, NB), jnp.float32)
    gram = lax.fori_loop(0, n_row, lambda i, g: g + dot(panel[i], panel[i], 0, 0), square)
    top = panel[0]
    left = Solve(False)
    left.first(gram)
    wait_all(sent_bw)
    sent_aw = start_all("row", n_row, row, lambda peer: aw.at[row], aw.at[row], s_aw)

    def products(ref):
        zero = jnp.zeros(ref.shape[1:], jnp.float32)
        return lax.fori_loop(0, n_row, lambda i, y: y + dot(ref[i], panel[i]), zero)

    left.second(gram, top)
    ready = left.prepare(products(bw), bw[0])
    left.third()
    coef_b = left.finish(*ready)
    strip = bw[n_row - 1] - dot(coef_b, panel[n_row - 1], 1, 1)
    strips[col] = strip
    spread_strips = Pairs(n_col, col, lambda c: strips.at[c], s_strips)
    spread_strips.start()

    v_rows = panel[row] + jnp.where(row == 0, left.factor(), 0.0)
    wait_all(sent_aw)
    sent_other = start_all("row", n_row, row, lambda peer: turned.at[peer], other.at[row], s_other)
    coef_a = left.finish(*left.prepare(products(aw), aw[0]))
    own = jnp.concatenate(
        [
            a_ref[:, start:] - dot(v_rows, coef_a, 1, 1),
            b_ref[:, start:] - dot(v_rows, coef_b, 1, 1),
        ],
        axis=0,
    )
    own_c[...] = own.reshape(own_c.shape)
    own_y[...] = dot(own, strip).reshape(own_y.shape)
    spread_strips.forward()
    sent_y = start_all("col", n_col, col, lambda peer: own_y.at[peer], got_y.at[col], s_y)
    place = col - (n_col - n_last)
    slot = jnp.maximum(place, 0)

    def last_copies():
        return [
            send(
                own_c.at[lax.rem(col + d, n_col)],
                got_c.at[slot],
                s_c[0].at[d - 1],
                s_c[1].at[slot],
                {"col": lax.rem(col + d, n_col)},
            )
            for d in range(1, n_col)
        ]

    @pl.when(place >= 0)
    def _():
        for copy in last_copies():
            copy.start()
        got_c[slot] = own_c[col]

    spread_strips.wait()

    def add(i, g):
        x = strips[pl.ds(i * n_last, n_last)].reshape(NB, NB)
        return g + dot(x, x, 0, 0)

    gram = lax.fori_loop(0, n_col // n_last, add, square)
    top = strips[n_col - n_last :].reshape(NB, NB)
    right = Solve(True)
    right.first(gram)

    wait_all(sent_y)
    for j in range(n_last):

        @pl.when(place != j)
        def _():
            source = n_col - n_last + j
            send(own_c.at[0], got_c.at[j], s_c[0].at[0], s_c[1].at[j], {"col": source}).wait_recv()

    @pl.when(place >= 0)
    def _():
        for copy in last_copies():
            copy.wait_send()

    total = own_y[col]
    for d in range(1, n_col):
        total = total + got_y[lax.rem(col + d, n_col)]
    both[col] = jnp.concatenate([total] + [got_c[j] for j in range(n_last)], axis=1)
    spread_both = Pairs(n_col, col, lambda c: both.at[c], s_both)
    spread_both.start()

    wait_all(sent_other)
    own_coefs = left.finish(*left.prepare(products(other), other[0]))
    coefs[row] = own_coefs
    sent_coefs = start_all("row", n_row, row, lambda peer: coefs.at[row], coefs.at[row], s_coefs)

    right.second(gram, top)
    spread_both.forward()
    right.third()
    r_ref[...] = right.factor()
    v_cols = strip + jnp.where(place >= 0, r_ref[pl.ds(slot * window, window), :], 0.0)

    wait_all(sent_coefs)
    all_coefs = coefs[...].reshape(2 * start, NB)
    oa_ref[:, :start] = a_ref[:, :start] - dot(v_rows, all_coefs[:start], 1, 1)
    ob_ref[:, :start] = b_ref[:, :start] - dot(v_rows, all_coefs[start:], 1, 1)

    spread_both.wait()
    sums = both[...].reshape(2 * rows, 2 * NB)
    coef = right.finish(*right.prepare(sums[:, :NB], sums[:, NB:]))
    done = own_c[...].reshape(2 * rows, window) - dot(coef, v_cols, 1, 1)
    oa_ref[:, start:] = done[:rows]
    ob_ref[:, start:] = done[rows:]


def local(a_matrix, b_matrix):
    rows, cols = a_matrix.shape
    n_row, n_col = lax.axis_size("row"), lax.axis_size("col")
    window = NB * n_row // n_col
    start = cols - window
    share, piece = 2 * rows // n_col, 2 * start // n_row
    f32 = jnp.float32

    def sems(sent, got=None):
        return [pltpu.SemaphoreType.DMA((sent,)), pltpu.SemaphoreType.DMA((got or sent,))]

    scratch = [
        pltpu.VMEM((n_row, rows, NB), f32),
        pltpu.VMEM((n_row, window, NB), f32),
        pltpu.VMEM((n_row, window, NB), f32),
        pltpu.VMEM((n_row, piece, NB), f32),
        pltpu.VMEM((n_row, piece, NB), f32),
        pltpu.VMEM((n_row, piece, NB), f32),
        pltpu.VMEM((n_col, window, NB), f32),
        pltpu.VMEM((n_col, share, NB), f32),
        pltpu.VMEM((n_col, share, NB), f32),
        pltpu.VMEM((n_col, share, window), f32),
        pltpu.VMEM((NB // window, share, window), f32),
        pltpu.VMEM((n_col, share, 2 * NB), f32),
        pltpu.VMEM((NB, NB), f32),
    ]
    scratch += sems(n_col - 1, 1) + sems(n_row - 1) + sems(n_col - 1)
    scratch += sems(n_row - 1) + sems(n_row - 1) + sems(n_row - 1) + sems(n_row - 1)
    scratch += sems(n_col - 1) + sems(n_col - 1) + sems(n_col - 1, NB // window) + sems(n_col - 1)
    out = jax.ShapeDtypeStruct((rows, cols), f32)
    return pl.pallas_call(
        functools.partial(kernel, n_row, n_col),
        out_shape=[out, out],
        in_specs=[VM, VM],
        out_specs=[VM, VM],
        scratch_shapes=scratch,
        compiler_params=pltpu.CompilerParams(
            collective_id=1, has_side_effects=True, vmem_limit_bytes=LIMIT
        ),
        name="reduction_step",
    )(a_matrix, b_matrix)


def solution(mesh):
    placed = (P("row", "col"), P("row", "col"))
    return jax.shard_map(
        lambda a, b: tuple(local(a, b)),
        mesh=mesh,
        in_specs=placed,
        out_specs=(P("row", "col"), P("row", "col")),
        check_vma=False,
    )
```

```python
import functools

import jax
import jax.numpy as jnp
from jax import lax
from jax.experimental import pallas as pl
from jax.experimental.pallas import tpu as pltpu
from jax.sharding import PartitionSpec as P

NB = 256
HB = NB // 2
TILE = 8
COUNT = HB // TILE
MESH = pl.DeviceIdType.MESH
VM = pl.BlockSpec(memory_space=pltpu.VMEM)
LIMIT = 32 * 1024 * 1024


def dot(x, y, cx=1, cy=0):
    return lax.dot_general(
        x,
        y,
        (((cx,), (cy,)), ((), ())),
        precision=lax.Precision.HIGHEST,
        preferred_element_type=jnp.float32,
    )


def spread(x):
    return jnp.broadcast_to(x, (TILE, HB))


def stack(rows):
    sub = lax.broadcasted_iota(jnp.int32, (TILE, HB), 0)
    out = rows[0]
    for k in range(1, TILE):
        out = jnp.where(sub == k, rows[k], out)
    return out


def apply_tile(tile, t, rows, inside):
    out = jnp.where(inside, 0.0, tile)
    for k in range(TILE):
        out = out - spread(tile[:, t * TILE + k : t * TILE + k + 1]) * rows[k]
    return out


def step(tiles, t, order, symmetric, room):
    lane = lax.broadcasted_iota(jnp.int32, (TILE, HB), 1) - t * TILE
    inside = (lane >= 0) & (lane < TILE)
    at = [lane == k for k in range(TILE)]
    place = {m: i for i, m in enumerate(order)}
    used = lambda r, k: not symmetric or place[r] <= place[k]
    rows = [spread(tiles[t][k : k + 1, :]) for k in range(TILE)]
    for k in range(TILE):
        room[k * TILE : (k + 1) * TILE, :] = spread(tiles[t][:, t * TILE + k : t * TILE + k + 1])
    s = [
        [
            spread(room[k * TILE + r : k * TILE + r + 1, :]) if used(r, k) else None
            for k in range(TILE)
        ]
        for r in range(TILE)
    ]
    rows = [jnp.where(inside, jnp.where(at[k], 1.0, 0.0), rows[k]) for k in range(TILE)]
    forward = [None] * TILE
    for i, m in enumerate(order):
        later = order[i + 1 :]
        if symmetric:
            kept = jnp.where(at[m], s[m][m], rows[m])
            for k in later:
                kept = jnp.where(at[k], s[m][k], kept)
            forward[m] = kept
        if symmetric and i % 2 == 0:
            n = order[i + 1]
            next_inv = s[m][m] * (1.0 / (s[m][m] * s[n][n] - s[m][n] * s[m][n]))
            inv = 1.0 / s[m][m]
        else:
            inv = next_inv if symmetric else 1.0 / s[m][m]
        lead = {r: s[m][r] if symmetric else s[r][m] for r in later}
        for k in later:
            s[m][k] = s[m][k] * inv
        for r in later:
            for k in later:
                if used(r, k):
                    s[r][k] = s[r][k] - lead[r] * s[m][k]
        rows[m] = rows[m] * inv
        for r in later:
            rows[r] = rows[r] - lead[r] * rows[m]
        yield None
    for i in range(TILE - 1, 0, -1):
        m = order[i]
        for r in order[:i]:
            rows[r] = rows[r] - s[r][m] * rows[m]
    yield rows, forward, inside


def invert_half(a, reverse, room):
    tiles = [a[i * TILE : (i + 1) * TILE, :] for i in range(COUNT)]
    order, places = list(range(TILE)), list(range(COUNT))
    if reverse:
        order, places = order[::-1], places[::-1]
    for n, t in enumerate(places):
        for out in step(tiles, t, order, False, room.at[t % 2]):
            yield None
        rows, _, inside = out
        new = list(tiles)
        for i in places[n + 1 :] + places[: n + 1]:
            new[i] = stack(rows) if i == t else apply_tile(tiles[i], t, rows, inside)
        tiles = new
        yield None
    yield jnp.concatenate(tiles, axis=0)


def eliminate_half(a, reverse, room):
    tiles = [a[i * TILE : (i + 1) * TILE, :] for i in range(COUNT)]
    order, places = list(range(TILE)), list(range(COUNT))
    if reverse:
        order, places = order[::-1], places[::-1]
    for n, t in enumerate(places):
        for out in step(tiles, t, order, True, room.at[2 + t % 2]):
            yield None
        rows, forward, inside = out
        tiles[t] = stack(forward)
        for i in places[n + 1 :]:
            tiles[i] = apply_tile(tiles[i], t, rows, inside)
        yield None
    a = jnp.concatenate(tiles, axis=0)
    rows = lax.broadcasted_iota(jnp.int32, (HB, HB), 0)
    cols = lax.broadcasted_iota(jnp.int32, (HB, HB), 1)
    diag = jnp.sum(jnp.where(rows == cols, a, 0.0), axis=1, keepdims=True)
    scale = 1.0 / jnp.sqrt(diag)
    keep = rows >= cols if reverse else rows <= cols
    factor = jnp.where(keep, a, 0.0) * scale
    yield factor, jnp.where(keep, jnp.where(rows == cols, 1.0, 0.0), a) * scale


def together(*chains):
    results, live = [None] * len(chains), list(range(len(chains)))
    while live:
        for j in list(live):
            value = next(chains[j], live)
            if value is live:
                live.remove(j)
            elif value is not None:
                results[j] = value
    return results


def after(count, action):
    for _ in range(count):
        yield None
    action()
    yield None


class Solve:
    def __init__(self, reverse, room):
        self.reverse, self.room = reverse, room
        self.p, self.q = (1, 0) if reverse else (0, 1)

    def cut(self, x, r, c):
        return x[r * HB : (r + 1) * HB, c * HB : (c + 1) * HB]

    def first(self, gram, *beside):
        p = self.p
        chain = eliminate_half(self.cut(gram, p, p), self.reverse, self.room)
        self.fpp, self.ipp = together(chain, *beside)[0]

    def second(self, gram, top, *beside):
        p, q = self.p, self.q
        self.rpq = dot(self.ipp, self.cut(gram, p, q))
        rest = self.cut(gram, q, q) - dot(self.rpq, self.rpq, 0, 0)
        (self.fqq, self.iqq), self.inv = together(
            eliminate_half(rest, self.reverse, self.room),
            invert_half(self.cut(top, p, p) + self.fpp, self.reverse, self.room),
            *beside,
        )[:2]
        self.fqp = self.cut(top, q, p)
        self.k = dot(self.inv, self.cut(top, p, q) + self.rpq)
        self.rest = self.cut(top, q, q) + self.fqq - dot(self.fqp, self.k)

    def third(self, *beside):
        results = together(invert_half(self.rest, self.reverse, self.room), *beside)
        self.sinv = results[0]
        return results[1:]

    def factor(self):
        zero = jnp.zeros((HB, HB), jnp.float32)
        if self.reverse:
            blocks = [[self.fqq, zero], [self.rpq, self.fpp]]
        else:
            blocks = [[self.fpp, self.rpq], [zero, self.fqq]]
        return jnp.concatenate([jnp.concatenate(b, axis=1) for b in blocks], axis=0)

    def prepare(self, y, t, gap=0):
        half = lambda x, i: x[:, i * HB : (i + 1) * HB]
        wait = [None] * gap
        yp = dot(half(y, self.p), self.ipp, 1, 1)
        yield from wait
        yq = half(y, self.q) - dot(yp, self.rpq)
        yield from wait
        yq = dot(yq, self.iqq, 1, 1)
        yield from wait
        hp = dot(yp + half(t, self.p), self.inv, 1, 1)
        yield from wait
        yield hp, yq + half(t, self.q) - dot(hp, self.fqp, 1, 1)

    def finish(self, hp, hq):
        cq = dot(hq, self.sinv, 1, 1)
        cp = hp - dot(cq, self.k, 1, 1)
        return jnp.concatenate([cq, cp] if self.reverse else [cp, cq], axis=1)


def send(source, target, send_sem, recv_sem, peer):
    copy = pltpu.make_async_remote_copy(
        src_ref=source,
        dst_ref=target,
        send_sem=send_sem,
        recv_sem=recv_sem,
        device_id=peer,
        device_id_type=MESH,
    )
    return copy


def start_all(axis, n, me, source, target, sems):
    copies = []
    for d in range(1, n):
        peer = lax.rem(me + d, n)
        copy = send(source(peer), target, sems[0].at[d - 1], sems[1].at[d - 1], {axis: peer})
        copy.start()
        copies.append(copy)
    return copies


def wait_all(copies):
    for copy in copies:
        copy.wait()


class Pairs:
    def __init__(self, n, me, slot, sems):
        self.n, self.me, self.slot, self.sems = n, me, slot, sems
        self.partner = me + 1 - 2 * lax.rem(me, 2)

    def copy(self, index, block, peer):
        ref = self.slot(block)
        copy = send(ref, ref, self.sems[0].at[index], self.sems[1].at[index], {"col": peer})
        copy.start()
        return copy

    def start(self):
        half = self.n // 2
        self.far = [
            self.copy(d - 1, self.me, lax.rem(self.me + 2 * d, self.n)) for d in range(1, half)
        ]
        self.near = [self.copy(half - 1, self.me, self.partner)]

    def forward(self):
        half = self.n // 2
        for d in range(1, half):
            self.far[d - 1].wait_recv()
            block = lax.rem(self.me + self.n - 2 * d, self.n)
            self.near.append(self.copy(half - 1 + d, block, self.partner))

    def wait(self):
        for copy in self.far:
            copy.wait_send()
        wait_all(self.near)


def kernel(n_row, n_col, a_ref, b_ref, oa_ref, ob_ref, *scratch):
    panel, bw, aw, turned, other, coefs, strips, own_y, got_y, own_c, got_c, both, r_ref, room = scratch[:14]
    pairs_of_sems = [scratch[i : i + 2] for i in range(14, len(scratch), 2)]
    s_scatter, s_row, s_panel, s_bw, s_aw, s_other, s_coefs, s_strips, s_y, s_c, s_both = pairs_of_sems
    rows, cols = a_ref.shape
    window = strips.shape[1]
    start = cols - window
    chunk = rows // n_col
    n_last = NB // window
    row, col = lax.axis_index("row"), lax.axis_index("col")

    barrier = pltpu.get_barrier_semaphore()
    for axis, n, me in (("row", n_row, row), ("col", n_col, col)):
        for d in range(1, n):
            pl.semaphore_signal(
                barrier, inc=1, device_id={axis: lax.rem(me + d, n)}, device_id_type=MESH
            )
    pl.semaphore_wait(barrier, n_row + n_col - 2)

    def part(c):
        return panel.at[row, pl.ds(c * chunk, chunk)]

    def scatter(c):
        source = a_ref.at[pl.ds(c * chunk, chunk), pl.ds(0, NB)]
        return send(source, part(c), s_scatter[0].at[c - 1], s_scatter[1].at[0], {"col": c})

    @pl.when(col == 0)
    def _():
        for c in range(1, n_col):
            scatter(c).start()
        panel[row, pl.ds(0, chunk)] = a_ref[:chunk, :NB]

    bw[row] = b_ref[:, start:].T
    aw[row] = a_ref[:, start:].T
    turned[...] = jnp.concatenate([a_ref[:, :start].T, b_ref[:, :start].T], axis=0).reshape(
        turned.shape
    )
    other[row] = turned[row]

    @pl.when(col != 0)
    def _():
        send(part(col), part(col), s_scatter[0].at[0], s_scatter[1].at[0], {"col": 0}).wait_recv()

    mine = part(col)
    chunks = start_all("row", n_row, row, lambda peer: mine, mine, s_row)
    sent_bw = start_all("row", n_row, row, lambda peer: bw.at[row], bw.at[row], s_bw)
    wait_all(chunks)
    spread_panel = Pairs(n_col, col, lambda c: panel.at[:, pl.ds(c * chunk, chunk)], s_panel)
    spread_panel.start()
    sent_aw = start_all("row", n_row, row, lambda peer: aw.at[row], aw.at[row], s_aw)
    spread_panel.forward()
    spread_panel.wait()

    @pl.when(col == 0)
    def _():
        for c in range(1, n_col):
            scatter(c).wait_send()

    square = jnp.zeros((NB, NB), jnp.float32)
    gram = lax.fori_loop(0, n_row, lambda i, g: g + dot(panel[i], panel[i], 0, 0), square)
    top = panel[0]
    left = Solve(False, room)
    left.first(gram)
    sent_other = start_all("row", n_row, row, lambda peer: turned.at[peer], other.at[row], s_other)
    left.second(gram, top)
    wait_all(sent_bw)

    def beside_third():
        y = dot(bw[0], panel[0])
        for i in range(1, n_row):
            yield from [None] * 8
            y = y + dot(bw[i], panel[i])
        yield from [None] * 8
        yield from left.prepare(y, bw[0], 12)

    coef_b = left.finish(*left.third(beside_third())[0])
    strip = bw[n_row - 1] - dot(coef_b, panel[n_row - 1], 1, 1)
    strips[col] = strip
    spread_strips = Pairs(n_col, col, lambda c: strips.at[c], s_strips)
    spread_strips.start()

    v_rows = panel[row] + jnp.where(row == 0, left.factor(), 0.0)
    wait_all(sent_aw)
    wait_all(sent_other)

    def products(i, y):
        return y + dot(jnp.concatenate([aw[i], other[i]], axis=0), panel[i])

    y = lax.fori_loop(0, n_row, products, jnp.zeros((window + turned.shape[1], NB), jnp.float32))
    (ready,) = together(left.prepare(y, jnp.concatenate([aw[0], other[0]], axis=0)))
    coef = left.finish(*ready)
    coefs[row] = coef[window:]
    sent_coefs = start_all("row", n_row, row, lambda peer: coefs.at[row], coefs.at[row], s_coefs)
    own = jnp.concatenate(
        [
            a_ref[:, start:] - dot(v_rows, coef[:window], 1, 1),
            b_ref[:, start:] - dot(v_rows, coef_b, 1, 1),
        ],
        axis=0,
    )
    own_c[...] = own.reshape(own_c.shape)
    own_y[...] = dot(own, strip).reshape(own_y.shape)
    spread_strips.forward()
    sent_y = start_all("col", n_col, col, lambda peer: own_y.at[peer], got_y.at[col], s_y)
    place = col - (n_col - n_last)
    slot = jnp.maximum(place, 0)

    def last_copies():
        return [
            send(
                own_c.at[lax.rem(col + d, n_col)],
                got_c.at[slot],
                s_c[0].at[d - 1],
                s_c[1].at[slot],
                {"col": lax.rem(col + d, n_col)},
            )
            for d in range(1, n_col)
        ]

    @pl.when(place >= 0)
    def _():
        for copy in last_copies():
            copy.start()
        got_c[slot] = own_c[col]

    spread_strips.wait()

    def add(i, g):
        x = strips[pl.ds(i * n_last, n_last)].reshape(NB, NB)
        return g + dot(x, x, 0, 0)

    gram = lax.fori_loop(0, n_col // n_last, add, square)
    top = strips[n_col - n_last :].reshape(NB, NB)
    right = Solve(True, room)
    spread_both = Pairs(n_col, col, lambda c: both.at[c], s_both)

    def reduce():
        wait_all(sent_y)
        for j in range(n_last):

            @pl.when(place != j)
            def _():
                source = n_col - n_last + j
                copy = send(own_c.at[0], got_c.at[j], s_c[0].at[0], s_c[1].at[j], {"col": source})
                copy.wait_recv()

        total = own_y[col]
        for d in range(1, n_col):
            total = total + got_y[lax.rem(col + d, n_col)]
        both[col] = jnp.concatenate([total] + [got_c[j] for j in range(n_last)], axis=1)
        spread_both.start()

    right.first(gram, after(10 * COUNT // 2, reduce))

    @pl.when(place >= 0)
    def _():
        for copy in last_copies():
            copy.wait_send()

    right.second(gram, top, after(10 * COUNT * 3 // 4, spread_both.forward))
    r_ref[...] = right.factor()
    v_cols = strip + jnp.where(place >= 0, r_ref[pl.ds(slot * window, window), :], 0.0)
    wait_all(sent_coefs)
    spread_both.wait()
    sums = both[...].reshape(2 * rows, 2 * NB)

    def outside():
        all_coefs = coefs[...].reshape(2 * start, NB)
        oa_ref[:, :start] = a_ref[:, :start] - dot(v_rows, all_coefs[:start], 1, 1)
        yield from [None] * 20
        ob_ref[:, :start] = b_ref[:, :start] - dot(v_rows, all_coefs[start:], 1, 1)
        yield None

    ready, _ = right.third(right.prepare(sums[:, :NB], sums[:, NB:], 20), outside())
    done = own_c[...].reshape(2 * rows, window) - dot(right.finish(*ready), v_cols, 1, 1)
    oa_ref[:, start:] = done[:rows]
    ob_ref[:, start:] = done[rows:]


def local(a_matrix, b_matrix):
    rows, cols = a_matrix.shape
    n_row, n_col = lax.axis_size("row"), lax.axis_size("col")
    window = NB * n_row // n_col
    start = cols - window
    share, piece = 2 * rows // n_col, 2 * start // n_row
    f32 = jnp.float32

    def sems(sent, got=None):
        return [pltpu.SemaphoreType.DMA((sent,)), pltpu.SemaphoreType.DMA((got or sent,))]

    scratch = [
        pltpu.VMEM((n_row, rows, NB), f32),
        pltpu.VMEM((n_row, window, NB), f32),
        pltpu.VMEM((n_row, window, NB), f32),
        pltpu.VMEM((n_row, piece, NB), f32),
        pltpu.VMEM((n_row, piece, NB), f32),
        pltpu.VMEM((n_row, piece, NB), f32),
        pltpu.VMEM((n_col, window, NB), f32),
        pltpu.VMEM((n_col, share, NB), f32),
        pltpu.VMEM((n_col, share, NB), f32),
        pltpu.VMEM((n_col, share, window), f32),
        pltpu.VMEM((NB // window, share, window), f32),
        pltpu.VMEM((n_col, share, 2 * NB), f32),
        pltpu.VMEM((NB, NB), f32),
        pltpu.VMEM((4, TILE * TILE, HB), f32),
    ]
    scratch += sems(n_col - 1, 1) + sems(n_row - 1) + sems(n_col - 1)
    scratch += sems(n_row - 1) + sems(n_row - 1) + sems(n_row - 1) + sems(n_row - 1)
    scratch += sems(n_col - 1) + sems(n_col - 1) + sems(n_col - 1, NB // window) + sems(n_col - 1)
    out = jax.ShapeDtypeStruct((rows, cols), f32)
    return pl.pallas_call(
        functools.partial(kernel, n_row, n_col),
        out_shape=[out, out],
        in_specs=[VM, VM],
        out_specs=[VM, VM],
        scratch_shapes=scratch,
        compiler_params=pltpu.CompilerParams(
            collective_id=1, has_side_effects=True, vmem_limit_bytes=LIMIT
        ),
        name="reduction_step",
    )(a_matrix, b_matrix)


def solution(mesh):
    placed = (P("row", "col"), P("row", "col"))
    return jax.shard_map(
        lambda a, b: tuple(local(a, b)),
        mesh=mesh,
        in_specs=placed,
        out_specs=(P("row", "col"), P("row", "col")),
        check_vma=False,
    )
```

```python
import functools

import jax
import jax.numpy as jnp
from jax import lax
from jax.experimental import pallas as pl
from jax.experimental.pallas import tpu as pltpu
from jax.sharding import PartitionSpec as P

NB = 256
HB = NB // 2
TILE = 8
COUNT = HB // TILE
MESH = pl.DeviceIdType.MESH
VM = pl.BlockSpec(memory_space=pltpu.VMEM)
LIMIT = 32 * 1024 * 1024


def dot(x, y, cx=1, cy=0):
    return lax.dot_general(
        x,
        y,
        (((cx,), (cy,)), ((), ())),
        precision=lax.Precision.HIGHEST,
        preferred_element_type=jnp.float32,
    )


def spread(x):
    return jnp.broadcast_to(x, (TILE, HB))


def stack(rows):
    sub = lax.broadcasted_iota(jnp.int32, (TILE, HB), 0)
    out = rows[0]
    for k in range(1, TILE):
        out = jnp.where(sub == k, rows[k], out)
    return out


def apply_tile(tile, t, rows, inside):
    out = jnp.where(inside, 0.0, tile)
    for k in range(TILE):
        out = out - spread(tile[:, t * TILE + k : t * TILE + k + 1]) * rows[k]
    return out


def step(tiles, t, order, symmetric, room):
    lane = lax.broadcasted_iota(jnp.int32, (TILE, HB), 1) - t * TILE
    inside = (lane >= 0) & (lane < TILE)
    at = [lane == k for k in range(TILE)]
    place = {m: i for i, m in enumerate(order)}
    used = lambda r, k: not symmetric or place[r] <= place[k]
    rows = [spread(tiles[t][k : k + 1, :]) for k in range(TILE)]
    for k in range(TILE):
        room[k * TILE : (k + 1) * TILE, :] = spread(tiles[t][:, t * TILE + k : t * TILE + k + 1])
    s = [
        [
            spread(room[k * TILE + r : k * TILE + r + 1, :]) if used(r, k) else None
            for k in range(TILE)
        ]
        for r in range(TILE)
    ]
    rows = [jnp.where(inside, jnp.where(at[k], 1.0, 0.0), rows[k]) for k in range(TILE)]
    forward = [None] * TILE
    for i, m in enumerate(order):
        later = order[i + 1 :]
        if symmetric:
            kept = jnp.where(at[m], s[m][m], rows[m])
            for k in later:
                kept = jnp.where(at[k], s[m][k], kept)
            forward[m] = kept
        if symmetric and i % 2 == 0:
            n = order[i + 1]
            next_inv = s[m][m] * (1.0 / (s[m][m] * s[n][n] - s[m][n] * s[m][n]))
            inv = 1.0 / s[m][m]
        else:
            inv = next_inv if symmetric else 1.0 / s[m][m]
        lead = {r: s[m][r] if symmetric else s[r][m] for r in later}
        for k in later:
            s[m][k] = s[m][k] * inv
        for r in later:
            for k in later:
                if used(r, k):
                    s[r][k] = s[r][k] - lead[r] * s[m][k]
        rows[m] = rows[m] * inv
        for r in later:
            rows[r] = rows[r] - lead[r] * rows[m]
        yield None
    for i in range(TILE - 1, 0, -1):
        m = order[i]
        for r in order[:i]:
            rows[r] = rows[r] - s[r][m] * rows[m]
    yield rows, forward, inside


def invert_half(a, reverse, room):
    tiles = [a[i * TILE : (i + 1) * TILE, :] for i in range(COUNT)]
    order, places = list(range(TILE)), list(range(COUNT))
    if reverse:
        order, places = order[::-1], places[::-1]
    for n, t in enumerate(places):
        for out in step(tiles, t, order, False, room.at[t % 2]):
            yield None
        rows, _, inside = out
        new = list(tiles)
        for i in places[n + 1 :] + places[: n + 1]:
            new[i] = stack(rows) if i == t else apply_tile(tiles[i], t, rows, inside)
        tiles = new
        yield None
    yield jnp.concatenate(tiles, axis=0)


def eliminate_half(a, reverse, room):
    tiles = [a[i * TILE : (i + 1) * TILE, :] for i in range(COUNT)]
    order, places = list(range(TILE)), list(range(COUNT))
    if reverse:
        order, places = order[::-1], places[::-1]
    for n, t in enumerate(places):
        for out in step(tiles, t, order, True, room.at[2 + t % 2]):
            yield None
        rows, forward, inside = out
        tiles[t] = stack(forward)
        for i in places[n + 1 :]:
            tiles[i] = apply_tile(tiles[i], t, rows, inside)
        yield None
    a = jnp.concatenate(tiles, axis=0)
    rows = lax.broadcasted_iota(jnp.int32, (HB, HB), 0)
    cols = lax.broadcasted_iota(jnp.int32, (HB, HB), 1)
    diag = jnp.sum(jnp.where(rows == cols, a, 0.0), axis=1, keepdims=True)
    scale = 1.0 / jnp.sqrt(diag)
    keep = rows >= cols if reverse else rows <= cols
    factor = jnp.where(keep, a, 0.0) * scale
    yield factor, jnp.where(keep, jnp.where(rows == cols, 1.0, 0.0), a) * scale


def together(*chains):
    results, live = [None] * len(chains), list(range(len(chains)))
    while live:
        for j in list(live):
            value = next(chains[j], live)
            if value is live:
                live.remove(j)
            elif value is not None:
                results[j] = value
    return results


def after(count, action):
    for _ in range(count):
        yield None
    action()
    yield None


class Solve:
    def __init__(self, reverse, room):
        self.reverse, self.room = reverse, room
        self.p, self.q = (1, 0) if reverse else (0, 1)

    def cut(self, x, r, c):
        return x[r * HB : (r + 1) * HB, c * HB : (c + 1) * HB]

    def first(self, gram, *beside):
        p = self.p
        chain = eliminate_half(self.cut(gram, p, p), self.reverse, self.room)
        self.fpp, self.ipp = together(chain, *beside)[0]

    def second(self, gram, top, *beside):
        p, q = self.p, self.q
        self.rpq = dot(self.ipp, self.cut(gram, p, q))
        rest = self.cut(gram, q, q) - dot(self.rpq, self.rpq, 0, 0)
        (self.fqq, self.iqq), self.inv = together(
            eliminate_half(rest, self.reverse, self.room),
            invert_half(self.cut(top, p, p) + self.fpp, self.reverse, self.room),
            *beside,
        )[:2]
        self.fqp = self.cut(top, q, p)
        self.k = dot(self.inv, self.cut(top, p, q) + self.rpq)
        self.rest = self.cut(top, q, q) + self.fqq - dot(self.fqp, self.k)

    def third(self, *beside):
        results = together(invert_half(self.rest, self.reverse, self.room), *beside)
        self.sinv = results[0]
        return results[1:]

    def factor(self):
        zero = jnp.zeros((HB, HB), jnp.float32)
        if self.reverse:
            blocks = [[self.fqq, zero], [self.rpq, self.fpp]]
        else:
            blocks = [[self.fpp, self.rpq], [zero, self.fqq]]
        return jnp.concatenate([jnp.concatenate(b, axis=1) for b in blocks], axis=0)

    def prepare(self, y, t, gap=0):
        half = lambda x, i: x[:, i * HB : (i + 1) * HB]
        wait = [None] * gap
        yp = dot(half(y, self.p), self.ipp, 1, 1)
        yield from wait
        yq = half(y, self.q) - dot(yp, self.rpq)
        yield from wait
        yq = dot(yq, self.iqq, 1, 1)
        yield from wait
        hp = dot(yp + half(t, self.p), self.inv, 1, 1)
        yield from wait
        yield hp, yq + half(t, self.q) - dot(hp, self.fqp, 1, 1)

    def finish(self, hp, hq):
        cq = dot(hq, self.sinv, 1, 1)
        cp = hp - dot(cq, self.k, 1, 1)
        return jnp.concatenate([cq, cp] if self.reverse else [cp, cq], axis=1)


def send(source, target, send_sem, recv_sem, peer):
    copy = pltpu.make_async_remote_copy(
        src_ref=source,
        dst_ref=target,
        send_sem=send_sem,
        recv_sem=recv_sem,
        device_id=peer,
        device_id_type=MESH,
    )
    return copy


def start_all(axis, n, me, source, target, sems):
    copies = []
    for d in range(1, n):
        peer = lax.rem(me + d, n)
        copy = send(source(peer), target, sems[0].at[d - 1], sems[1].at[d - 1], {axis: peer})
        copy.start()
        copies.append(copy)
    return copies


def wait_all(copies):
    for copy in copies:
        copy.wait()


class Pairs:
    def __init__(self, n, me, slot, sems):
        self.n, self.me, self.slot, self.sems = n, me, slot, sems
        self.partner = me + 1 - 2 * lax.rem(me, 2)

    def copy(self, index, block, peer):
        ref = self.slot(block)
        copy = send(ref, ref, self.sems[0].at[index], self.sems[1].at[index], {"col": peer})
        copy.start()
        return copy

    def start(self):
        half = self.n // 2
        self.far = [
            self.copy(d - 1, self.me, lax.rem(self.me + 2 * d, self.n)) for d in range(1, half)
        ]
        self.near = [self.copy(half - 1, self.me, self.partner)]

    def forward(self, use=None):
        half = self.n // 2
        for d in range(1, half):
            self.far[d - 1].wait_recv()
            block = lax.rem(self.me + self.n - 2 * d, self.n)
            self.near.append(self.copy(half - 1 + d, block, self.partner))
            if use is not None:
                use(block)

    def wait(self, use=None):
        for d, copy in enumerate(self.near):
            copy.wait_recv()
            if use is not None:
                use(lax.rem(self.partner + self.n - 2 * d, self.n))
        for copy in self.far + self.near:
            copy.wait_send()


class Gram:
    def __init__(self, ref):
        self.ref, self.total = ref, None

    def __call__(self, c):
        x = self.ref(c)[...].reshape(-1, NB)
        part = dot(x, x, 0, 0)
        self.total = part if self.total is None else self.total + part


def kernel(n_row, n_col, a_hbm, b_hbm, oa_ref, ob_ref, *scratch):
    a_ref, b_ref, loaded, own_y, pair_y, sum_y, got_y, s_pair, *scratch = scratch
    panel, bw, aw, turned, other, coefs, strips, own_c, got_c, both, r_ref, room = scratch[:12]
    pairs_of_sems = [scratch[i : i + 2] for i in range(12, len(scratch), 2)]
    s_scatter, s_row, s_panel, s_bw, s_aw, s_other, s_coefs, s_strips, s_y, s_c, s_both = pairs_of_sems
    rows, cols = a_ref.shape
    window = strips.shape[1]
    start = cols - window
    chunk = rows // n_col
    n_last = NB // window
    row, col = lax.axis_index("row"), lax.axis_index("col")

    barrier = pltpu.get_barrier_semaphore()
    for axis, n, me in (("row", n_row, row), ("col", n_col, col)):
        for d in range(1, n):
            pl.semaphore_signal(
                barrier, inc=1, device_id={axis: lax.rem(me + d, n)}, device_id_type=MESH
            )
    loads = [
        pltpu.make_async_copy(source, target, loaded.at[i])
        for i, (source, target) in enumerate([(a_hbm, a_ref), (b_hbm, b_ref)])
    ]
    for copy in loads:
        copy.start()
    for copy in loads:
        copy.wait()
    bw[row] = b_ref[:, start:].T
    aw[row] = a_ref[:, start:].T
    turned[...] = jnp.concatenate([a_ref[:, :start].T, b_ref[:, :start].T], axis=0).reshape(
        turned.shape
    )
    other[row] = turned[row]
    pl.semaphore_wait(barrier, n_row + n_col - 2)

    def part(c):
        return panel.at[row, pl.ds(c * chunk, chunk)]

    def scatter(c):
        source = a_ref.at[pl.ds(c * chunk, chunk), pl.ds(0, NB)]
        return send(source, part(c), s_scatter[0].at[c - 1], s_scatter[1].at[0], {"col": c})

    @pl.when(col == 0)
    def _():
        for c in range(1, n_col):
            scatter(c).start()
        panel[row, pl.ds(0, chunk)] = a_ref[:chunk, :NB]

    @pl.when(col != 0)
    def _():
        send(part(col), part(col), s_scatter[0].at[0], s_scatter[1].at[0], {"col": 0}).wait_recv()

    mine = part(col)
    chunks = start_all("row", n_row, row, lambda peer: mine, mine, s_row)
    sent_bw = start_all("row", n_row, row, lambda peer: bw.at[row], bw.at[row], s_bw)
    wait_all(chunks)
    block = lambda c: panel.at[:, pl.ds(pl.multiple_of(c * chunk, chunk), chunk)]
    spread_panel = Pairs(n_col, col, block, s_panel)
    spread_panel.start()
    sent_aw = start_all("row", n_row, row, lambda peer: aw.at[row], aw.at[row], s_aw)
    gram = Gram(block)
    gram(col)
    spread_panel.forward(gram)
    spread_panel.wait(gram)

    @pl.when(col == 0)
    def _():
        for c in range(1, n_col):
            scatter(c).wait_send()

    gram = gram.total
    top = panel[0]
    left = Solve(False, room)
    left.first(gram)
    sent_other = start_all("row", n_row, row, lambda peer: turned.at[peer], other.at[row], s_other)
    left.second(gram, top)
    wait_all(sent_bw)

    def beside_third():
        y = dot(bw[0], panel[0])
        for i in range(1, n_row):
            yield from [None] * 8
            y = y + dot(bw[i], panel[i])
        yield from [None] * 8
        yield from left.prepare(y, bw[0], 12)

    coef_b = left.finish(*left.third(beside_third())[0])
    strip = bw[n_row - 1] - dot(coef_b, panel[n_row - 1], 1, 1)
    strips[col] = strip
    spread_strips = Pairs(n_col, col, lambda c: strips.at[c], s_strips)
    spread_strips.start()

    v_rows = panel[row] + jnp.where(row == 0, left.factor(), 0.0)

    def products(ref):
        zero = jnp.zeros(ref.shape[1:], jnp.float32)
        return lax.fori_loop(0, n_row, lambda i, y: y + dot(ref[i], panel[i]), zero)

    def coefficients(ref):
        (ready,) = together(left.prepare(products(ref), ref[0]))
        return left.finish(*ready)

    wait_all(sent_aw)
    own = jnp.concatenate(
        [
            a_ref[:, start:] - dot(v_rows, coefficients(aw), 1, 1),
            b_ref[:, start:] - dot(v_rows, coef_b, 1, 1),
        ],
        axis=0,
    )
    own_c[...] = own.reshape(own_c.shape)
    own_y[...] = dot(own, strip).reshape(own_y.shape)

    n_chip, chip, core = n_col // 2, col // 2, lax.rem(col, 2)
    pair = send(
        own_y.at[:, 1 - core], pair_y, s_pair.at[0], s_pair.at[1], {"col": col + 1 - 2 * core}
    )
    pair.start()
    wait_all(sent_other)
    coefs[row] = coefficients(other)
    sent_coefs = start_all("row", n_row, row, lambda peer: coefs.at[row], coefs.at[row], s_coefs)
    pair.wait()
    sum_y[...] = own_y[:, core] + pair_y[...]
    gram = Gram(lambda c: strips.at[c])
    gram(col)
    spread_strips.forward(gram)
    sent_y = []
    for d in range(1, n_chip):
        to = lax.rem(chip + d, n_chip)
        copy = send(
            sum_y.at[to], got_y.at[chip], s_y[0].at[d - 1], s_y[1].at[d - 1], {"col": 2 * to + core}
        )
        copy.start()
        sent_y.append(copy)
    place = col - (n_col - n_last)
    slot = jnp.maximum(place, 0)

    def last_copies():
        return [
            send(
                own_c.at[lax.rem(col + d, n_col)],
                got_c.at[slot],
                s_c[0].at[d - 1],
                s_c[1].at[slot],
                {"col": lax.rem(col + d, n_col)},
            )
            for d in range(1, n_col)
        ]

    @pl.when(place >= 0)
    def _():
        for copy in last_copies():
            copy.start()
        got_c[slot] = own_c[col]

    spread_strips.wait(gram)
    gram = gram.total
    top = strips[n_col - n_last :].reshape(NB, NB)
    right = Solve(True, room)
    spread_both = Pairs(n_col, col, lambda c: both.at[c], s_both)

    def reduce():
        wait_all(sent_y)
        for j in range(n_last):

            @pl.when(place != j)
            def _():
                source = n_col - n_last + j
                copy = send(own_c.at[0], got_c.at[j], s_c[0].at[0], s_c[1].at[j], {"col": source})
                copy.wait_recv()

        total = sum_y[chip]
        for d in range(1, n_chip):
            total = total + got_y[lax.rem(chip + d, n_chip)]
        both[col] = jnp.concatenate([total] + [got_c[j] for j in range(n_last)], axis=1)
        spread_both.start()

    right.first(gram, after(10 * COUNT // 2, reduce))

    @pl.when(place >= 0)
    def _():
        for copy in last_copies():
            copy.wait_send()

    right.second(gram, top, after(10 * COUNT * 3 // 4, spread_both.forward))
    r_ref[...] = right.factor()
    v_cols = strip + jnp.where(place >= 0, r_ref[pl.ds(slot * window, window), :], 0.0)
    wait_all(sent_coefs)
    spread_both.wait()
    sums = both[...].reshape(2 * rows, 2 * NB)

    def outside():
        all_coefs = coefs[...].reshape(2 * start, NB)
        oa_ref[:, :start] = a_ref[:, :start] - dot(v_rows, all_coefs[:start], 1, 1)
        yield from [None] * 20
        ob_ref[:, :start] = b_ref[:, :start] - dot(v_rows, all_coefs[start:], 1, 1)
        yield None

    ready, _ = right.third(right.prepare(sums[:, :NB], sums[:, NB:], 20), outside())
    done = own_c[...].reshape(2 * rows, window) - dot(right.finish(*ready), v_cols, 1, 1)
    oa_ref[:, start:] = done[:rows]
    ob_ref[:, start:] = done[rows:]


def local(a_matrix, b_matrix):
    rows, cols = a_matrix.shape
    n_row, n_col = lax.axis_size("row"), lax.axis_size("col")
    window = NB * n_row // n_col
    start = cols - window
    share, piece = 2 * rows // n_col, 2 * start // n_row
    f32 = jnp.float32

    def sems(sent, got=None):
        return [pltpu.SemaphoreType.DMA((sent,)), pltpu.SemaphoreType.DMA((got or sent,))]

    scratch = [
        pltpu.VMEM((rows, cols), f32),
        pltpu.VMEM((rows, cols), f32),
        pltpu.SemaphoreType.DMA((2,)),
        pltpu.VMEM((n_col // 2, 2, share, NB), f32),
        pltpu.VMEM((n_col // 2, share, NB), f32),
        pltpu.VMEM((n_col // 2, share, NB), f32),
        pltpu.VMEM((n_col // 2, share, NB), f32),
        pltpu.SemaphoreType.DMA((2,)),
        pltpu.VMEM((n_row, rows, NB), f32),
        pltpu.VMEM((n_row, window, NB), f32),
        pltpu.VMEM((n_row, window, NB), f32),
        pltpu.VMEM((n_row, piece, NB), f32),
        pltpu.VMEM((n_row, piece, NB), f32),
        pltpu.VMEM((n_row, piece, NB), f32),
        pltpu.VMEM((n_col, window, NB), f32),
        pltpu.VMEM((n_col, share, window), f32),
        pltpu.VMEM((NB // window, share, window), f32),
        pltpu.VMEM((n_col, share, 2 * NB), f32),
        pltpu.VMEM((NB, NB), f32),
        pltpu.VMEM((4, TILE * TILE, HB), f32),
    ]
    scratch += sems(n_col - 1, 1) + sems(n_row - 1) + sems(n_col - 1)
    scratch += sems(n_row - 1) + sems(n_row - 1) + sems(n_row - 1) + sems(n_row - 1)
    scratch += sems(n_col - 1) + sems(n_col // 2 - 1) + sems(n_col - 1, NB // window) + sems(n_col - 1)
    out = jax.ShapeDtypeStruct((rows, cols), f32)
    return pl.pallas_call(
        functools.partial(kernel, n_row, n_col),
        out_shape=[out, out],
        in_specs=[pl.BlockSpec(memory_space=pltpu.HBM)] * 2,
        out_specs=[VM, VM],
        scratch_shapes=scratch,
        compiler_params=pltpu.CompilerParams(
            collective_id=1, has_side_effects=True, vmem_limit_bytes=LIMIT
        ),
        name="reduction_step",
    )(*(pltpu.with_memory_space_constraint(x, pltpu.HBM) for x in (a_matrix, b_matrix)))


def solution(mesh):
    placed = (P("row", "col"), P("row", "col"))
    return jax.shard_map(
        lambda a, b: tuple(local(a, b)),
        mesh=mesh,
        in_specs=placed,
        out_specs=(P("row", "col"), P("row", "col")),
        check_vma=False,
    )
```

```python
import functools

import jax
import jax.numpy as jnp
from jax import lax
from jax.experimental import pallas as pl
from jax.experimental.pallas import tpu as pltpu
from jax.sharding import PartitionSpec as P

NB = 256
HB = NB // 2
TILE = 8
COUNT = HB // TILE
MESH = pl.DeviceIdType.MESH
VM = pl.BlockSpec(memory_space=pltpu.VMEM)
LIMIT = 32 * 1024 * 1024


def dot(x, y, cx=1, cy=0):
    return lax.dot_general(
        x,
        y,
        (((cx,), (cy,)), ((), ())),
        precision=lax.Precision.HIGHEST,
        preferred_element_type=jnp.float32,
    )


def spread(x):
    return jnp.broadcast_to(x, (TILE, HB))


def stack(rows):
    sub = lax.broadcasted_iota(jnp.int32, (TILE, HB), 0)
    out = rows[0]
    for k in range(1, TILE):
        out = jnp.where(sub == k, rows[k], out)
    return out


def apply_tile(tile, t, rows, inside):
    out = jnp.where(inside, 0.0, tile)
    for k in range(TILE):
        out = out - spread(tile[:, t * TILE + k : t * TILE + k + 1]) * rows[k]
    return out


def step(tiles, t, order, symmetric, room):
    lane = lax.broadcasted_iota(jnp.int32, (TILE, HB), 1) - t * TILE
    inside = (lane >= 0) & (lane < TILE)
    at = [lane == k for k in range(TILE)]
    place = {m: i for i, m in enumerate(order)}
    used = lambda r, k: not symmetric or place[r] <= place[k]
    rows = [spread(tiles[t][k : k + 1, :]) for k in range(TILE)]
    for k in range(TILE):
        room[k * TILE : (k + 1) * TILE, :] = spread(tiles[t][:, t * TILE + k : t * TILE + k + 1])
    s = [
        [
            spread(room[k * TILE + r : k * TILE + r + 1, :]) if used(r, k) else None
            for k in range(TILE)
        ]
        for r in range(TILE)
    ]
    rows = [jnp.where(inside, jnp.where(at[k], 1.0, 0.0), rows[k]) for k in range(TILE)]
    forward = [None] * TILE
    for i, m in enumerate(order):
        later = order[i + 1 :]
        if symmetric:
            kept = jnp.where(at[m], s[m][m], rows[m])
            for k in later:
                kept = jnp.where(at[k], s[m][k], kept)
            forward[m] = kept
        if symmetric and i % 2 == 0:
            n = order[i + 1]
            next_inv = s[m][m] * (1.0 / (s[m][m] * s[n][n] - s[m][n] * s[m][n]))
            inv = 1.0 / s[m][m]
        else:
            inv = next_inv if symmetric else 1.0 / s[m][m]
        lead = {r: s[m][r] if symmetric else s[r][m] for r in later}
        for k in later:
            s[m][k] = s[m][k] * inv
        for r in later:
            for k in later:
                if used(r, k):
                    s[r][k] = s[r][k] - lead[r] * s[m][k]
        rows[m] = rows[m] * inv
        for r in later:
            rows[r] = rows[r] - lead[r] * rows[m]
        yield None
    for i in range(TILE - 1, 0, -1):
        m = order[i]
        for r in order[:i]:
            rows[r] = rows[r] - s[r][m] * rows[m]
    yield rows, forward, inside


def invert_half(a, reverse, room):
    tiles = [a[i * TILE : (i + 1) * TILE, :] for i in range(COUNT)]
    order, places = list(range(TILE)), list(range(COUNT))
    if reverse:
        order, places = order[::-1], places[::-1]
    for n, t in enumerate(places):
        for out in step(tiles, t, order, False, room.at[t % 2]):
            yield None
        rows, _, inside = out
        new = list(tiles)
        for i in places[n + 1 :] + places[: n + 1]:
            new[i] = stack(rows) if i == t else apply_tile(tiles[i], t, rows, inside)
        tiles = new
        yield None
    yield jnp.concatenate(tiles, axis=0)


def eliminate_half(a, reverse, room):
    tiles = [a[i * TILE : (i + 1) * TILE, :] for i in range(COUNT)]
    order, places = list(range(TILE)), list(range(COUNT))
    if reverse:
        order, places = order[::-1], places[::-1]
    for n, t in enumerate(places):
        for out in step(tiles, t, order, True, room.at[2 + t % 2]):
            yield None
        rows, forward, inside = out
        tiles[t] = stack(forward)
        for i in places[n + 1 :]:
            tiles[i] = apply_tile(tiles[i], t, rows, inside)
        yield None
    a = jnp.concatenate(tiles, axis=0)
    rows = lax.broadcasted_iota(jnp.int32, (HB, HB), 0)
    cols = lax.broadcasted_iota(jnp.int32, (HB, HB), 1)
    diag = jnp.sum(jnp.where(rows == cols, a, 0.0), axis=1, keepdims=True)
    scale = 1.0 / jnp.sqrt(diag)
    keep = rows >= cols if reverse else rows <= cols
    factor = jnp.where(keep, a, 0.0) * scale
    yield factor, jnp.where(keep, jnp.where(rows == cols, 1.0, 0.0), a) * scale


def together(*chains):
    results, live = [None] * len(chains), list(range(len(chains)))
    while live:
        for j in list(live):
            value = next(chains[j], live)
            if value is live:
                live.remove(j)
            elif value is not None:
                results[j] = value
    return results


def after(count, action):
    for _ in range(count):
        yield None
    action()
    yield None


class Solve:
    def __init__(self, reverse, room):
        self.reverse, self.room = reverse, room
        self.p, self.q = (1, 0) if reverse else (0, 1)

    def cut(self, x, r, c):
        return x[r * HB : (r + 1) * HB, c * HB : (c + 1) * HB]

    def first(self, gram, *beside):
        p = self.p
        chain = eliminate_half(self.cut(gram, p, p), self.reverse, self.room)
        self.fpp, self.ipp = together(chain, *beside)[0]

    def second(self, gram, top, *beside):
        p, q = self.p, self.q
        self.rpq = dot(self.ipp, self.cut(gram, p, q))
        rest = self.cut(gram, q, q) - dot(self.rpq, self.rpq, 0, 0)
        (self.fqq, self.iqq), self.inv = together(
            eliminate_half(rest, self.reverse, self.room),
            invert_half(self.cut(top, p, p) + self.fpp, self.reverse, self.room),
            *beside,
        )[:2]
        self.fqp = self.cut(top, q, p)
        self.k = dot(self.inv, self.cut(top, p, q) + self.rpq)
        self.rest = self.cut(top, q, q) + self.fqq - dot(self.fqp, self.k)

    def third(self, *beside):
        results = together(invert_half(self.rest, self.reverse, self.room), *beside)
        self.sinv = results[0]
        return results[1:]

    def factor(self):
        zero = jnp.zeros((HB, HB), jnp.float32)
        if self.reverse:
            blocks = [[self.fqq, zero], [self.rpq, self.fpp]]
        else:
            blocks = [[self.fpp, self.rpq], [zero, self.fqq]]
        return jnp.concatenate([jnp.concatenate(b, axis=1) for b in blocks], axis=0)

    def prepare(self, y, t, gap=0):
        half = lambda x, i: x[:, i * HB : (i + 1) * HB]
        wait = [None] * gap
        yp = dot(half(y, self.p), self.ipp, 1, 1)
        yield from wait
        yq = half(y, self.q) - dot(yp, self.rpq)
        yield from wait
        yq = dot(yq, self.iqq, 1, 1)
        yield from wait
        hp = dot(yp + half(t, self.p), self.inv, 1, 1)
        yield from wait
        yield hp, yq + half(t, self.q) - dot(hp, self.fqp, 1, 1)

    def finish(self, hp, hq):
        cq = dot(hq, self.sinv, 1, 1)
        cp = hp - dot(cq, self.k, 1, 1)
        return jnp.concatenate([cq, cp] if self.reverse else [cp, cq], axis=1)


def send(source, target, send_sem, recv_sem, peer):
    copy = pltpu.make_async_remote_copy(
        src_ref=source,
        dst_ref=target,
        send_sem=send_sem,
        recv_sem=recv_sem,
        device_id=peer,
        device_id_type=MESH,
    )
    return copy


def start_all(axis, n, me, source, target, sems):
    copies = []
    for d in range(1, n):
        peer = lax.rem(me + d, n)
        copy = send(source(peer), target, sems[0].at[d - 1], sems[1].at[d - 1], {axis: peer})
        copy.start()
        copies.append(copy)
    return copies


def wait_all(copies):
    for copy in copies:
        copy.wait()


class Pairs:
    def __init__(self, n, me, slot, sems):
        self.n, self.me, self.slot, self.sems = n, me, slot, sems
        self.partner = me + 1 - 2 * lax.rem(me, 2)

    def copy(self, index, block, peer):
        ref = self.slot(block)
        copy = send(ref, ref, self.sems[0].at[index], self.sems[1].at[index], {"col": peer})
        copy.start()
        return copy

    def start(self):
        half = self.n // 2
        self.far = [
            self.copy(d - 1, self.me, lax.rem(self.me + 2 * d, self.n)) for d in range(1, half)
        ]
        self.near = [self.copy(half - 1, self.me, self.partner)]

    def forward(self, use=None):
        half = self.n // 2
        for d in range(1, half):
            self.far[d - 1].wait_recv()
            block = lax.rem(self.me + self.n - 2 * d, self.n)
            self.near.append(self.copy(half - 1 + d, block, self.partner))
            if use is not None:
                use(block)

    def wait(self, use=None):
        for d, copy in enumerate(self.near):
            copy.wait_recv()
            if use is not None:
                use(lax.rem(self.partner + self.n - 2 * d, self.n))
        for copy in self.far + self.near:
            copy.wait_send()


class Gram:
    def __init__(self, ref):
        self.ref, self.total = ref, None

    def __call__(self, c):
        x = self.ref(c)[...].reshape(-1, NB)
        part = dot(x, x, 0, 0)
        self.total = part if self.total is None else self.total + part


def kernel(n_row, n_col, a_hbm, b_hbm, oa_ref, ob_ref, *scratch):
    a_ref, b_ref, loaded, own_y, pair_y, sum_y, got_y, s_pair, *scratch = scratch
    panel, bw, aw, turned, other, coefs, strips, own_c, got_c, both, r_ref, room = scratch[:12]
    pairs_of_sems = [scratch[i : i + 2] for i in range(12, len(scratch), 2)]
    s_scatter, s_row, s_panel, s_bw, s_aw, s_other, s_coefs, s_strips, s_y, s_c, s_both = pairs_of_sems
    rows, cols = a_ref.shape
    window = strips.shape[1]
    start = cols - window
    chunk = rows // n_col
    n_last = NB // window
    row, col = lax.axis_index("row"), lax.axis_index("col")

    barrier = pltpu.get_barrier_semaphore()
    for axis, n, me in (("row", n_row, row), ("col", n_col, col)):
        for d in range(1, n):
            pl.semaphore_signal(
                barrier, inc=1, device_id={axis: lax.rem(me + d, n)}, device_id_type=MESH
            )
    loads = [
        pltpu.make_async_copy(source, target, loaded.at[i])
        for i, (source, target) in enumerate([(a_hbm, a_ref), (b_hbm, b_ref)])
    ]
    for copy in loads:
        copy.start()
    for copy in loads:
        copy.wait()
    bw[row] = b_ref[:, start:].T
    aw[row] = a_ref[:, start:].T
    turned[...] = jnp.concatenate([a_ref[:, :start].T, b_ref[:, :start].T], axis=0).reshape(
        turned.shape
    )
    other[row] = turned[row]
    pl.semaphore_wait(barrier, n_row + n_col - 2)

    def part(c):
        return panel.at[row, pl.ds(c * chunk, chunk)]

    def scatter(c):
        source = a_ref.at[pl.ds(c * chunk, chunk), pl.ds(0, NB)]
        return send(source, part(c), s_scatter[0].at[c - 1], s_scatter[1].at[0], {"col": c})

    @pl.when(col == 0)
    def _():
        for c in range(1, n_col):
            scatter(c).start()
        panel[row, pl.ds(0, chunk)] = a_ref[:chunk, :NB]

    @pl.when(col != 0)
    def _():
        send(part(col), part(col), s_scatter[0].at[0], s_scatter[1].at[0], {"col": 0}).wait_recv()

    mine = part(col)
    chunks = start_all("row", n_row, row, lambda peer: mine, mine, s_row)
    sent_bw = start_all("row", n_row, row, lambda peer: bw.at[row], bw.at[row], s_bw)
    block = lambda c: panel.at[:, pl.ds(pl.multiple_of(c * chunk, chunk), chunk)]
    spreads = []
    for d in range(n_row):
        if d:
            chunks[d - 1].wait_recv()
        slot = lambda c, r=lax.rem(row + n_row - d, n_row): panel.at[r, pl.ds(c * chunk, chunk)]
        spreads.append(Pairs(n_col, col, slot, [s.at[d] for s in s_panel]))
        spreads[d].start()
    sent_aw = start_all("row", n_row, row, lambda peer: aw.at[row], aw.at[row], s_aw)
    gram = Gram(block)
    gram(col)
    for each in spreads:
        each.forward()
    for d in range(1, n_col // 2):
        gram(lax.rem(col + n_col - 2 * d, n_col))
    for d in range(n_col // 2):
        for each in spreads:
            each.near[d].wait_recv()
        gram(lax.rem(each.partner + n_col - 2 * d, n_col))
    for each in spreads:
        for copy in each.far + each.near:
            copy.wait_send()
    for copy in chunks:
        copy.wait_send()

    @pl.when(col == 0)
    def _():
        for c in range(1, n_col):
            scatter(c).wait_send()

    gram = gram.total
    top = panel[0]
    left = Solve(False, room)
    left.first(gram)
    sent_other = start_all("row", n_row, row, lambda peer: turned.at[peer], other.at[row], s_other)
    left.second(gram, top)
    wait_all(sent_bw)

    def beside_third():
        y = dot(bw[0], panel[0])
        for i in range(1, n_row):
            yield from [None] * 8
            y = y + dot(bw[i], panel[i])
        yield from [None] * 8
        yield from left.prepare(y, bw[0], 12)

    coef_b = left.finish(*left.third(beside_third())[0])
    strip = bw[n_row - 1] - dot(coef_b, panel[n_row - 1], 1, 1)
    strips[col] = strip
    spread_strips = Pairs(n_col, col, lambda c: strips.at[c], s_strips)
    spread_strips.start()

    v_rows = panel[row] + jnp.where(row == 0, left.factor(), 0.0)

    def products(ref):
        zero = jnp.zeros(ref.shape[1:], jnp.float32)
        return lax.fori_loop(0, n_row, lambda i, y: y + dot(ref[i], panel[i]), zero)

    def coefficients(ref):
        (ready,) = together(left.prepare(products(ref), ref[0]))
        return left.finish(*ready)

    wait_all(sent_aw)
    own = jnp.concatenate(
        [
            a_ref[:, start:] - dot(v_rows, coefficients(aw), 1, 1),
            b_ref[:, start:] - dot(v_rows, coef_b, 1, 1),
        ],
        axis=0,
    )
    own_c[...] = own.reshape(own_c.shape)
    own_y[...] = dot(own, strip).reshape(own_y.shape)

    n_chip, chip, core = n_col // 2, col // 2, lax.rem(col, 2)
    pair = send(
        own_y.at[:, 1 - core], pair_y, s_pair.at[0], s_pair.at[1], {"col": col + 1 - 2 * core}
    )
    pair.start()
    wait_all(sent_other)
    coefs[row] = coefficients(other)
    sent_coefs = start_all("row", n_row, row, lambda peer: coefs.at[row], coefs.at[row], s_coefs)
    pair.wait()
    sum_y[...] = own_y[:, core] + pair_y[...]
    gram = Gram(lambda c: strips.at[c])
    gram(col)
    spread_strips.forward(gram)
    sent_y = []
    for d in range(1, n_chip):
        to = lax.rem(chip + d, n_chip)
        copy = send(
            sum_y.at[to], got_y.at[chip], s_y[0].at[d - 1], s_y[1].at[d - 1], {"col": 2 * to + core}
        )
        copy.start()
        sent_y.append(copy)
    place = col - (n_col - n_last)
    slot = jnp.maximum(place, 0)

    def last_copies():
        return [
            send(
                own_c.at[lax.rem(col + d, n_col)],
                got_c.at[slot],
                s_c[0].at[d - 1],
                s_c[1].at[slot],
                {"col": lax.rem(col + d, n_col)},
            )
            for d in range(1, n_col)
        ]

    @pl.when(place >= 0)
    def _():
        for copy in last_copies():
            copy.start()
        got_c[slot] = own_c[col]

    spread_strips.wait(gram)
    gram = gram.total
    top = strips[n_col - n_last :].reshape(NB, NB)
    right = Solve(True, room)
    spread_both = Pairs(n_col, col, lambda c: both.at[c], s_both)

    def reduce():
        wait_all(sent_y)
        for j in range(n_last):

            @pl.when(place != j)
            def _():
                source = n_col - n_last + j
                copy = send(own_c.at[0], got_c.at[j], s_c[0].at[0], s_c[1].at[j], {"col": source})
                copy.wait_recv()

        total = sum_y[chip]
        for d in range(1, n_chip):
            total = total + got_y[lax.rem(chip + d, n_chip)]
        sums.extend([total, jnp.concatenate([got_c[j] for j in range(n_last)], axis=1)])

    sums = []
    right.first(gram)

    @pl.when(place >= 0)
    def _():
        for copy in last_copies():
            copy.wait_send()

    right.second(gram, top, after(10 * COUNT // 2, reduce))
    (ready,) = together(right.prepare(*sums))
    both[col] = jnp.concatenate(ready, axis=1)
    spread_both.start()
    r_ref[...] = right.factor()
    v_cols = strip + jnp.where(place >= 0, r_ref[pl.ds(slot * window, window), :], 0.0)
    wait_all(sent_coefs)

    def outside():
        all_coefs = coefs[...].reshape(2 * start, NB)
        oa_ref[:, :start] = a_ref[:, :start] - dot(v_rows, all_coefs[:start], 1, 1)
        yield from [None] * 20
        ob_ref[:, :start] = b_ref[:, :start] - dot(v_rows, all_coefs[start:], 1, 1)
        yield None

    right.third(outside())
    spread_both.forward()
    spread_both.wait()
    ready = both[...].reshape(2 * rows, NB)
    coef = right.finish(ready[:, :HB], ready[:, HB:])
    done = own_c[...].reshape(2 * rows, window) - dot(coef, v_cols, 1, 1)
    oa_ref[:, start:] = done[:rows]
    ob_ref[:, start:] = done[rows:]


def local(a_matrix, b_matrix):
    rows, cols = a_matrix.shape
    n_row, n_col = lax.axis_size("row"), lax.axis_size("col")
    window = NB * n_row // n_col
    start = cols - window
    share, piece = 2 * rows // n_col, 2 * start // n_row
    f32 = jnp.float32

    def sems(sent, got=None):
        return [pltpu.SemaphoreType.DMA((sent,)), pltpu.SemaphoreType.DMA((got or sent,))]

    scratch = [
        pltpu.VMEM((rows, cols), f32),
        pltpu.VMEM((rows, cols), f32),
        pltpu.SemaphoreType.DMA((2,)),
        pltpu.VMEM((n_col // 2, 2, share, NB), f32),
        pltpu.VMEM((n_col // 2, share, NB), f32),
        pltpu.VMEM((n_col // 2, share, NB), f32),
        pltpu.VMEM((n_col // 2, share, NB), f32),
        pltpu.SemaphoreType.DMA((2,)),
        pltpu.VMEM((n_row, rows, NB), f32),
        pltpu.VMEM((n_row, window, NB), f32),
        pltpu.VMEM((n_row, window, NB), f32),
        pltpu.VMEM((n_row, piece, NB), f32),
        pltpu.VMEM((n_row, piece, NB), f32),
        pltpu.VMEM((n_row, piece, NB), f32),
        pltpu.VMEM((n_col, window, NB), f32),
        pltpu.VMEM((n_col, share, window), f32),
        pltpu.VMEM((NB // window, share, window), f32),
        pltpu.VMEM((n_col, share, NB), f32),
        pltpu.VMEM((NB, NB), f32),
        pltpu.VMEM((4, TILE * TILE, HB), f32),
    ]
    scratch += sems(n_col - 1, 1) + sems(n_row - 1)
    scratch += [pltpu.SemaphoreType.DMA((n_row, n_col - 1))] * 2
    scratch += sems(n_row - 1) + sems(n_row - 1) + sems(n_row - 1) + sems(n_row - 1)
    scratch += sems(n_col - 1) + sems(n_col // 2 - 1) + sems(n_col - 1, NB // window) + sems(n_col - 1)
    out = jax.ShapeDtypeStruct((rows, cols), f32)
    return pl.pallas_call(
        functools.partial(kernel, n_row, n_col),
        out_shape=[out, out],
        in_specs=[pl.BlockSpec(memory_space=pltpu.HBM)] * 2,
        out_specs=[VM, VM],
        scratch_shapes=scratch,
        compiler_params=pltpu.CompilerParams(
            collective_id=1, has_side_effects=True, vmem_limit_bytes=LIMIT
        ),
        name="reduction_step",
    )(*(pltpu.with_memory_space_constraint(x, pltpu.HBM) for x in (a_matrix, b_matrix)))


def solution(mesh):
    placed = (P("row", "col"), P("row", "col"))
    return jax.shard_map(
        lambda a, b: tuple(local(a, b)),
        mesh=mesh,
        in_specs=placed,
        out_specs=(P("row", "col"), P("row", "col")),
        check_vma=False,
    )
```
